512 devices in a mesh: cam: 16 (over z_lo, x), seq: 32 (over y, z_hi, core).
Axes of the slice: x: 4, y: 4, z: 16 (z_hi: 4, z_lo: 4; z = z_hi * 4 + z_lo), core: 2. Of those that a mesh axis runs over, the one named last changes fastest.
Arguments:
- queries: bfloat16 [16, 2048, 2048], P('cam', 'seq'), may hold values from -18 to 18
- keys: bfloat16 [16, 2048, 2048], P('cam', 'seq'), may hold values from -8 to 8
- values: bfloat16 [16, 2048, 2048], P('cam', 'seq'), may hold values from -6 to 6
- neighbour_mask: int32 [16, 4], replicated, may hold values from 0 to 1, as said below
Outputs:
- attended: bfloat16 [16, 2048, 2048], P('cam', 'seq')
The draws below stay inside these ranges and needn't reach their ends.
Inputs may be any that keep to these rules, and one draw needn't show every extreme that they name: `neighbour_mask`: at least one camera has all 4 neighbours.
All inputs are finite; a program needn't handle non-finite values.
Results may differ from the reference program's by a relative error of at most 0.012.
Values may be sent and summed in bfloat16 or wider, within the bound.
No kernel may reach another device: no remote copies, remote signals or barrier semaphores. Data moves between devices by JAX's collectives and lax.ppermute only.
A program may use at most 64 MiB of HBM per device.

```python
import math
from functools import reduce
import jax
import jax.numpy as jnp
from jax import lax

D = 2048
HEADS = 32
HD = 64
VIEW_TOKENS = 2048
CAMS = 16
REACH = 2
NOFF = 4


def draw_queries(key, part):
    key = jax.random.fold_in(key, 1)
    first_key = jax.random.fold_in(key, 0)
    filled = jnp.clip(jax.random.normal(first_key, (CAMS, VIEW_TOKENS, D), jnp.float32) * 2.5, -12.0, 12.0)
    return filled.astype(jnp.bfloat16)


def draw_keys(key, part):
    key = jax.random.fold_in(key, 2)
    first_key = jax.random.fold_in(key, 0)
    filled = jnp.clip(jax.random.normal(first_key, (CAMS, VIEW_TOKENS, D), jnp.float32), -6.0, 6.0)
    return filled.astype(jnp.bfloat16)


def draw_neighbour_mask(key, part):
    key = jax.random.fold_in(key, 7)
    first_key, second_key = jax.random.split(key)
    chosen = jax.random.randint(first_key, (CAMS, NOFF), 0, 2)
    busiest = jax.random.randint(second_key, (), 0, CAMS)
    return jnp.where(jnp.arange(CAMS)[:, None] == busiest, 1, chosen).astype(jnp.int32)


def levels(stream_key, dims, cuts, least, top_value):
    def one(position, blocks):
        steps = jax.random.uniform(jax.random.fold_in(jax.random.fold_in(stream_key, 6), position), (blocks,), jnp.float32, least / len(cuts), top_value / len(cuts))
        return jnp.repeat(jnp.exp(steps), dims[position] // blocks).reshape((-1,) + (1,) * (len(dims) - position - 1))

    level = one(*cuts[0])
    for cut in cuts[1:]:
        level = level * one(*cut)
    return level


def noise(rng, dims, scale, reach, pieces=(), kind=jnp.bfloat16):
    gain = levels(rng, dims, pieces, -0.22, 0.18) if pieces else 1.0
    result = jax.random.normal(rng, dims, jnp.float32) * scale * gain
    return jnp.minimum(jnp.maximum(result, -reach), reach).astype(kind)


def setup_inputs(seed: int = 0) -> dict:
    key_list = jax.random.split(jax.random.key(seed), 5)
    return {
        "queries": draw_queries(jax.random.fold_in(key_list[4], 71), 0),
        "keys": draw_keys(jax.random.fold_in(key_list[4], 71), 0),
        "values": noise(key_list[2], (CAMS, VIEW_TOKENS, D), 1.0, 6.0, ((0, 16), (1, 32))),
        "neighbour_mask": draw_neighbour_mask(jax.random.fold_in(key_list[4], 71), 0),
    }


def attend_view(queries, keys, values):
    length, head_count, head_width = queries.shape
    block_rows = math.gcd(length, 512)
    score_scale = head_width ** -0.5
    keys_wide = keys.astype(jnp.float32)
    values_wide = values.astype(jnp.float32)

    def one_block(query_rows):
        scores = jnp.einsum("bhd,khd->hbk", query_rows.astype(jnp.float32), keys_wide, precision=lax.Precision.HIGHEST) * score_scale
        highest = jnp.max(scores, axis=2)
        exponent = jnp.exp(scores - highest[:, :, None])
        totals = jnp.sum(exponent, axis=2)
        weights = lax.optimization_barrier(exponent.astype(jnp.bfloat16)).astype(jnp.float32)
        blended = jnp.einsum("hbk,khd->bhd", weights, values_wide, precision=lax.Precision.HIGHEST)
        blended = (blended / totals.T[:, :, None]).astype(jnp.bfloat16)
        return blended, highest.T, totals.T

    grouped = queries.reshape(length // block_rows, block_rows, head_count, head_width)
    blended, highest, totals = lax.map(one_block, grouped)
    return (blended.reshape(length, head_count, head_width), highest.reshape(length, head_count), totals.reshape(length, head_count))


def maybe_attend(enabled, queries, keys, values):
    length, head_count, head_width = queries.shape

    def skipped():
        return (jnp.zeros((length, head_count, head_width), jnp.bfloat16), jnp.zeros((length, head_count), jnp.float32), jnp.zeros((length, head_count), jnp.float32))

    return lax.cond(enabled > 0, lambda: attend_view(queries, keys, values), skipped)


def merge_blocks(members, markers):
    peaks = [jnp.where(marker > 0, member[1], -jnp.inf) for member, marker in zip(members, markers)]
    highest = reduce(jnp.maximum, peaks)
    numerator = jnp.zeros(members[0][0].shape, jnp.float32)
    denominator = jnp.zeros(highest.shape, jnp.float32)
    for member, marker, peak_value in zip(members, markers, peaks):
        weight = jnp.where(marker > 0, member[2] * jnp.exp(peak_value - highest), 0.0)
        numerator = numerator + weight[:, :, None] * member[0].astype(jnp.float32)
        denominator = denominator + weight
    return (numerator / denominator[:, :, None]).astype(jnp.bfloat16)


def reference(queries, keys, values, neighbour_mask):
    offsets = [distance for distance in range(1, REACH + 1)] + [-distance for distance in range(1, REACH + 1)]

    def one_camera(camera):
        own_queries = queries[camera].reshape(VIEW_TOKENS, HEADS, HD)
        members = [attend_view(own_queries, keys[camera].reshape(VIEW_TOKENS, HEADS, HD), values[camera].reshape(VIEW_TOKENS, HEADS, HD))]
        markers = [jnp.int32(1)]
        for column, offset in enumerate(offsets):
            other = ((camera + offset) % CAMS).astype(jnp.int32)
            enabled = neighbour_mask[camera, column]
            members.append(maybe_attend(enabled, own_queries, keys[other].reshape(VIEW_TOKENS, HEADS, HD), values[other].reshape(VIEW_TOKENS, HEADS, HD)))
            markers.append(enabled)
        return merge_blocks(members, markers).reshape(VIEW_TOKENS, D)

    return lax.map(one_camera, jnp.arange(CAMS, dtype=jnp.int32))
```

```python
import functools

import jax
import jax.numpy as jnp
from jax import lax
from jax.experimental import pallas as pl
from jax.experimental.pallas import tpu as pltpu
from jax.sharding import PartitionSpec as P

HEADS = 32
HD = 64
WIDE = 2 * HD
TILE = 256

VMEM = pl.BlockSpec(memory_space=pltpu.VMEM)
SMEM = pl.BlockSpec(memory_space=pltpu.SMEM)


def params(mib):
    return pltpu.CompilerParams(vmem_limit_bytes=mib << 20)


def pack_pairs_kernel(left_ref, right_ref, out_ref):
    for pair in range(HEADS // 2):
        left = left_ref[:, pair * WIDE : (pair + 1) * WIDE]
        right = right_ref[:, pair * WIDE : (pair + 1) * WIDE]
        out_ref[2 * pair] = jnp.concatenate([left[:, :HD], right[:, :HD]], axis=1)
        out_ref[2 * pair + 1] = jnp.concatenate([left[:, HD:], right[:, HD:]], axis=1)


def pack_keys_values(keys, values):
    rows = keys.shape[0]
    return pl.pallas_call(
        pack_pairs_kernel,
        out_shape=jax.ShapeDtypeStruct((HEADS, rows, WIDE), keys.dtype),
        in_specs=[VMEM, VMEM],
        out_specs=VMEM,
        compiler_params=params(16),
        name="pack_keys_values",
    )(keys, values)


def pack_queries_kernel(q_ref, out_ref):
    half = q_ref.shape[0] // 2
    pack_pairs_kernel(q_ref.at[pl.ds(0, half)], q_ref.at[pl.ds(half, half)], out_ref)


def pack_queries(queries):
    rows = queries.shape[0]
    return pl.pallas_call(
        pack_queries_kernel,
        out_shape=jax.ShapeDtypeStruct((HEADS, rows // 2, WIDE), queries.dtype),
        in_specs=[VMEM],
        out_specs=VMEM,
        compiler_params=params(16),
        name="pack_queries",
    )(queries)


def unpack_kernel(x_ref, out_ref):
    half = x_ref.shape[1]
    for pair in range(HEADS // 2):
        even, odd = x_ref[2 * pair], x_ref[2 * pair + 1]
        columns = pl.ds(pair * WIDE, WIDE)
        out_ref[pl.ds(0, half), columns] = jnp.concatenate([even[:, :HD], odd[:, :HD]], axis=1)
        out_ref[pl.ds(half, half), columns] = jnp.concatenate([even[:, HD:], odd[:, HD:]], axis=1)


def unpack_heads(x):
    return pl.pallas_call(
        unpack_kernel,
        out_shape=jax.ShapeDtypeStruct((2 * x.shape[1], HEADS * HD), x.dtype),
        in_specs=[VMEM],
        out_specs=VMEM,
        compiler_params=params(16),
        name="unpack_heads",
    )(x)


def tile_scores(q_ref, half, rows, keys):
    queries = q_ref[rows, half * HD : (half + 1) * HD] * jnp.bfloat16(HD**-0.5)
    return lax.dot_general(queries, keys, (((1,), (1,)), ((), ())), preferred_element_type=jnp.float32)


def halves(kv_ref):
    kv = kv_ref[...]
    lane = lax.broadcasted_iota(jnp.int32, kv.shape, 1)
    return kv[:, :HD], jnp.where(lane < HD, jnp.bfloat16(1), kv)


def tiles(q_ref):
    for start in range(0, q_ref.shape[0], TILE):
        for half in range(2):
            yield pl.ds(start, TILE), half


def first_kernel(q_ref, kv_ref, sums_ref, peaks_ref):
    keys, values = halves(kv_ref)
    for rows, half in tiles(q_ref):
        scores = tile_scores(q_ref, half, rows, keys)
        peak = jnp.max(scores, axis=1, keepdims=True)
        weights = jnp.exp(scores - peak).astype(jnp.bfloat16)
        sums_ref[half, rows] = jnp.dot(weights, values, preferred_element_type=jnp.float32)
        peaks_ref[half, rows] = jnp.broadcast_to(peak, (TILE, WIDE))


def next_kernel(column, enabled_ref, q_ref, kv_ref, old_sums_ref, old_peaks_ref, sums_ref, peaks_ref):
    @pl.when(enabled_ref[column] > 0)
    def _():
        keys, values = halves(kv_ref)
        for rows, half in tiles(q_ref):
            scores = tile_scores(q_ref, half, rows, keys)
            old_peak = old_peaks_ref[half, rows]
            peak = jnp.maximum(jnp.max(scores, axis=1, keepdims=True), old_peak)
            weights = jnp.exp(scores - peak[:, :1]).astype(jnp.bfloat16)
            added = jnp.dot(weights, values, preferred_element_type=jnp.float32)
            sums_ref[half, rows] = old_sums_ref[half, rows] * jnp.exp(old_peak - peak) + added
            peaks_ref[half, rows] = peak


def last_kernel(column, enabled_ref, q_ref, kv_ref, old_sums_ref, old_peaks_ref, out_ref):
    def store(rows, half, sums):
        out_ref[rows, half * HD : (half + 1) * HD] = (sums[:, HD:] / sums[:, :HD]).astype(out_ref.dtype)

    @pl.when(enabled_ref[column] > 0)
    def _():
        keys, values = halves(kv_ref)
        for rows, half in tiles(q_ref):
            scores = tile_scores(q_ref, half, rows, keys)
            old_peak = old_peaks_ref[half, rows]
            peak = jnp.maximum(jnp.max(scores, axis=1, keepdims=True), old_peak)
            weights = jnp.exp(scores - peak[:, :1]).astype(jnp.bfloat16)
            added = jnp.dot(weights, values, preferred_element_type=jnp.float32)
            store(rows, half, old_sums_ref[half, rows] * jnp.exp(old_peak - peak) + added)

    @pl.when(enabled_ref[column] <= 0)
    def _():
        for rows, half in tiles(q_ref):
            store(rows, half, old_sums_ref[half, rows])


def cost(q, kv):
    pairs = 2 * q.shape[0] * kv.shape[0]
    return pl.CostEstimate(flops=4 * pairs * HD, bytes_accessed=3 << 20, transcendentals=pairs)


def state_shape(q):
    return jax.ShapeDtypeStruct((2, q.shape[0], WIDE), jnp.float32)


def first_block(q, kv):
    return pl.pallas_call(
        first_kernel,
        out_shape=(state_shape(q), state_shape(q)),
        in_specs=[VMEM, VMEM],
        out_specs=(VMEM, VMEM),
        compiler_params=params(40),
        cost_estimate=cost(q, kv),
        name="own_camera",
    )(q, kv)


def next_block(column, enabled, q, kv, sums, peaks):
    return pl.pallas_call(
        functools.partial(next_kernel, column),
        out_shape=(state_shape(q), state_shape(q)),
        in_specs=[SMEM, VMEM, VMEM, VMEM, VMEM],
        out_specs=(VMEM, VMEM),
        input_output_aliases={3: 0, 4: 1},
        compiler_params=params(40),
        cost_estimate=cost(q, kv),
        name="next_camera",
    )(enabled, q, kv, sums, peaks)


def last_block(column, enabled, q, kv, sums, peaks):
    return pl.pallas_call(
        functools.partial(last_kernel, column),
        out_shape=jax.ShapeDtypeStruct(q.shape, q.dtype),
        in_specs=[SMEM, VMEM, VMEM, VMEM, VMEM],
        out_specs=VMEM,
        compiler_params=params(40),
        cost_estimate=cost(q, kv),
        name="last_camera",
    )(enabled, q, kv, sums, peaks)


def shifted(array, axis, by):
    devices = lax.axis_size(axis)
    return lax.ppermute(array, axis, [(i, (i + by) % devices) for i in range(devices)])


def on_device(queries, keys, values, neighbour_mask):
    own_row = lax.dynamic_index_in_dim(neighbour_mask, lax.axis_index("cam"), 0, keepdims=False)
    kv = pack_keys_values(keys[0], values[0])
    kv = lax.all_to_all(kv, "seq", split_axis=0, concat_axis=0, tiled=True).reshape(-1, WIDE)
    q = pack_queries(queries[0])
    shape = q.shape
    q = lax.all_to_all(q, "seq", split_axis=0, concat_axis=0, tiled=True).reshape(-1, WIDE)
    far = [shifted(kv, "cam", -1), shifted(kv, "cam", -2), shifted(kv, "cam", 1), shifted(kv, "cam", 2)]
    sums, peaks = first_block(q, kv)
    for column in (0, 2, 1):
        sums, peaks = next_block(column, own_row, q, far[column], sums, peaks)
    out = last_block(3, own_row, q, far[3], sums, peaks).reshape(shape)
    out = lax.all_to_all(out, "seq", split_axis=0, concat_axis=0, tiled=True)
    return unpack_heads(out)[None]


def solution(mesh):
    return jax.shard_map(
        on_device,
        mesh=mesh,
        in_specs=(P("cam", "seq", None), P("cam", "seq", None), P("cam", "seq", None), P()),
        out_specs=P("cam", "seq", None),
        check_vma=False,
    )
```

```python
import functools

import jax
import jax.numpy as jnp
from jax import lax
from jax.experimental import pallas as pl
from jax.experimental.pallas import tpu as pltpu
from jax.sharding import PartitionSpec as P

HEADS = 32
HD = 64
WIDE = 2 * HD
TILE = 256
QROWS = 32
LOWEST = -1e30

VMEM = pl.BlockSpec(memory_space=pltpu.VMEM)
SMEM = pl.BlockSpec(memory_space=pltpu.SMEM)


def params(mib):
    return pltpu.CompilerParams(vmem_limit_bytes=mib << 20)


CHUNKS = 4


def side_by_side(out_ref, rows, head, left, right):
    out_ref[head, rows] = jnp.concatenate([left[:, :HD], right[:, :HD]], axis=1)
    out_ref[head + 1, rows] = jnp.concatenate([left[:, HD:], right[:, HD:]], axis=1)


def pack_kernel(q_hbm, k_hbm, v_hbm, out_ref, q_ref, k_ref, v_ref, arrived):
    tokens, width = q_ref.shape
    step = width // CHUNKS
    copies = []
    for chunk in range(CHUNKS):
        columns = pl.ds(chunk * step, step)
        for place, (far, near) in enumerate(((k_hbm, k_ref), (v_hbm, v_ref), (q_hbm, q_ref))):
            copy = pltpu.make_async_copy(far.at[:, columns], near.at[:, columns], arrived.at[chunk, place])
            copy.start()
            copies.append(copy)
    half = tokens // 2
    for chunk in range(CHUNKS):
        for copy in copies[3 * chunk : 3 * chunk + 3]:
            copy.wait()
        for start in range(chunk * step, (chunk + 1) * step, WIDE):
            columns = pl.ds(start, WIDE)
            head = start // HD
            side_by_side(out_ref, pl.ds(0, tokens), head, k_ref[:, columns], v_ref[:, columns])
            upper, lower = q_ref[pl.ds(0, half), columns], q_ref[pl.ds(half, half), columns]
            side_by_side(out_ref, pl.ds(tokens, half), head, upper, lower)


def pack_heads(queries, keys, values):
    tokens, width = keys.shape
    held = pltpu.VMEM((tokens, width), keys.dtype)
    return pl.pallas_call(
        pack_kernel,
        out_shape=jax.ShapeDtypeStruct((HEADS, tokens + tokens // 2, WIDE), keys.dtype),
        in_specs=[pl.BlockSpec(memory_space=pl.ANY)] * 3,
        out_specs=VMEM,
        scratch_shapes=[held, held, held, pltpu.SemaphoreType.DMA((CHUNKS, 3))],
        compiler_params=params(60),
        name="pack_heads",
    )(queries, keys, values)


def unpack_kernel(x_ref, out_ref):
    half = x_ref.shape[1]
    for pair in range(HEADS // 2):
        even, odd = x_ref[2 * pair], x_ref[2 * pair + 1]
        columns = pl.ds(pair * WIDE, WIDE)
        out_ref[pl.ds(0, half), columns] = jnp.concatenate([even[:, :HD], odd[:, :HD]], axis=1)
        out_ref[pl.ds(half, half), columns] = jnp.concatenate([even[:, HD:], odd[:, HD:]], axis=1)


def unpack_heads(x):
    return pl.pallas_call(
        unpack_kernel,
        out_shape=jax.ShapeDtypeStruct((2 * x.shape[1], HEADS * HD), x.dtype),
        in_specs=[VMEM],
        out_specs=VMEM,
        compiler_params=params(16),
        name="unpack_heads",
    )(x)


def tile_scores(packed_ref, rows, half, keys):
    sources = TILE // QROWS
    queries = packed_ref[rows // QROWS : rows // QROWS + sources, 2 * QROWS :, half * HD : (half + 1) * HD]
    queries = queries.reshape(TILE, HD) * jnp.bfloat16(HD**-0.5)
    return lax.dot_general(queries, keys, (((1,), (1,)), ((), ())), preferred_element_type=jnp.float32)


def keys_and_values(kv):
    lane = lax.broadcasted_iota(jnp.int32, kv.shape, 1)
    return kv[:, :HD], jnp.where(lane < HD, jnp.bfloat16(1), kv)


def attend(packed_ref, kv_ref, old_peaks, store):
    keys, values = keys_and_values(kv_ref[...])
    units = [(rows, half) for rows in range(0, packed_ref.shape[0] * QROWS, TILE) for half in range(2)]

    def blend(rows, half, peak, old_peak, weights):
        store(rows, half, peak, old_peak, jnp.dot(weights, values, preferred_element_type=jnp.float32))

    scores = tile_scores(packed_ref, *units[0], keys)
    waiting = None
    for place, (rows, half) in enumerate(units):
        ahead = tile_scores(packed_ref, *units[place + 1], keys) if place + 1 < len(units) else None
        peak = jnp.max(scores, axis=1, keepdims=True)
        old_peak = None
        if old_peaks is not None:
            old_peak = old_peaks[half, pl.ds(rows, TILE)]
            peak = jnp.maximum(peak, old_peak)
        weights = jnp.exp(scores - peak[:, :1]).astype(jnp.bfloat16)
        if waiting is not None:
            blend(*waiting)
        waiting = (rows, half, peak, old_peak, weights)
        scores = ahead
    blend(*waiting)


def update(packed_ref, kv_ref, old_sums, old_peaks, sums, peaks):
    def store(rows, half, peak, old_peak, added):
        rows = pl.ds(rows, TILE)
        if old_peak is not None:
            added = old_sums[half, rows] * jnp.exp(old_peak - peak) + added
        sums[half, rows] = added
        peaks[half, rows] = jnp.broadcast_to(peak, (TILE, WIDE))

    attend(packed_ref, kv_ref, old_peaks, store)


def own_kernel(packed_ref, kv_ref, sums, peaks, mark):
    update(packed_ref, kv_ref, None, None, sums, peaks)
    mark[...] = jnp.zeros_like(mark)


def near_kernel(columns, mask_ref, packed_ref, one_ref, two_ref, _, sums, peaks):
    @pl.when(mask_ref[columns[0]] > 0)
    def _():
        update(packed_ref, one_ref, None, None, sums, peaks)

    @pl.when(mask_ref[columns[0]] <= 0)
    def _():
        sums[...] = jnp.zeros_like(sums)
        peaks[...] = jnp.full_like(peaks, LOWEST)

    @pl.when(mask_ref[columns[1]] > 0)
    def _():
        update(packed_ref, two_ref, sums, peaks, sums, peaks)


def far_kernel(
    columns, mask_ref, packed_ref, one_ref, two_ref, own_sums, own_peaks, near_sums, near_peaks, out_ref, sums, peaks
):
    @pl.when(mask_ref[columns[0]] > 0)
    def _():
        update(packed_ref, one_ref, near_sums, near_peaks, sums, peaks)

    @pl.when(mask_ref[columns[0]] <= 0)
    def _():
        sums[...] = near_sums[...]
        peaks[...] = near_peaks[...]

    def finish(rows, half, parts):
        parts = parts + [(own_sums[half, rows], own_peaks[half, rows]), (sums[half, rows], peaks[half, rows])]
        highest = functools.reduce(jnp.maximum, [part[1] for part in parts])
        total = sum(part[0] * jnp.exp(part[1] - highest) for part in parts)
        out_ref[rows, half * HD : (half + 1) * HD] = (total[:, HD:] / total[:, :HD]).astype(out_ref.dtype)

    def store(rows, half, peak, old_peak, added):
        finish(pl.ds(rows, TILE), half, [(added, jnp.broadcast_to(peak, added.shape))])

    @pl.when(mask_ref[columns[1]] > 0)
    def _():
        attend(packed_ref, two_ref, None, store)

    @pl.when(mask_ref[columns[1]] <= 0)
    def _():
        for start in range(0, out_ref.shape[0], TILE):
            for half in range(2):
                finish(pl.ds(start, TILE), half, [])


def cost(packed, blocks):
    pairs = blocks * (packed.shape[0] * 2 * QROWS) ** 2
    return pl.CostEstimate(flops=4 * pairs * HD, bytes_accessed=3 << 20, transcendentals=pairs)


def state_shape(packed):
    return jax.ShapeDtypeStruct((2, packed.shape[0] * QROWS, WIDE), jnp.float32)


def own_camera(packed, kv):
    return pl.pallas_call(
        own_kernel,
        out_shape=(state_shape(packed), state_shape(packed), jax.ShapeDtypeStruct((8, WIDE), jnp.float32)),
        in_specs=[VMEM, VMEM],
        out_specs=(VMEM, VMEM, VMEM),
        compiler_params=params(32),
        cost_estimate=cost(packed, 1),
        name="own_camera",
    )(packed, kv)


def near_cameras(columns, mask, packed, one, two, mark):
    return pl.pallas_call(
        functools.partial(near_kernel, columns),
        out_shape=(state_shape(packed), state_shape(packed)),
        in_specs=[SMEM] + [VMEM] * 4,
        out_specs=(VMEM, VMEM),
        compiler_params=params(32),
        cost_estimate=cost(packed, 2),
        name="near_cameras",
    )(mask, packed, one, two, mark)


def far_cameras(columns, mask, packed, one, two, own, near):
    state = pltpu.VMEM(near[0].shape, near[0].dtype)
    return pl.pallas_call(
        functools.partial(far_kernel, columns),
        out_shape=jax.ShapeDtypeStruct((near[0].shape[1], WIDE), packed.dtype),
        in_specs=[SMEM] + [VMEM] * 7,
        out_specs=VMEM,
        scratch_shapes=[state, state],
        compiler_params=params(32),
        cost_estimate=cost(packed, 2),
        name="far_cameras",
    )(mask, packed, one, two, *own, *near)


def swapped(array, axis, first):
    devices = lax.axis_size(axis)
    pairs = [(i % devices, (i + 1) % devices) for i in range(first, first + devices, 2)]
    return lax.ppermute(array, axis, pairs + [(j, i) for i, j in pairs])


def on_device(queries, keys, values, neighbour_mask):
    camera = lax.axis_index("cam")
    own_row = lax.dynamic_index_in_dim(neighbour_mask, camera, 0, keepdims=False)
    own_row = jnp.where(camera % 2 == 0, own_row, jnp.roll(own_row, 2))
    packed = pack_heads(queries[0], keys[0], values[0])
    packed = lax.all_to_all(packed, "seq", split_axis=0, concat_axis=0, tiled=True)
    kv = packed[:, : 2 * QROWS].reshape(-1, WIDE)
    one, two = swapped(kv, "cam", 0), swapped(kv, "cam", 1)
    *own, mark = own_camera(packed, kv)
    one, mark = lax.optimization_barrier((one, mark))
    far_two, far_one = swapped(one, "cam", 1), swapped(two, "cam", 0)
    near = near_cameras((0, 2), own_row, packed, one, two, mark)
    out = far_cameras((3, 1), own_row, packed, far_two, far_one, own, near)
    out = out.reshape(HEADS, QROWS, WIDE)
    out = lax.all_to_all(out, "seq", split_axis=0, concat_axis=0, tiled=True)
    return unpack_heads(out)[None]


def solution(mesh):
    return jax.shard_map(
        on_device,
        mesh=mesh,
        in_specs=(P("cam", "seq", None), P("cam", "seq", None), P("cam", "seq", None), P()),
        out_specs=P("cam", "seq", None),
        check_vma=False,
    )
```

```python
import functools

import jax
import jax.numpy as jnp
from jax import lax
from jax.experimental import pallas as pl
from jax.experimental.pallas import tpu as pltpu
from jax.sharding import PartitionSpec as P

HEADS = 32
HD = 64
WIDE = 2 * HD
TILE = 256
QROWS = 32
LOWEST = -1e30

VMEM = pl.BlockSpec(memory_space=pltpu.VMEM)
SMEM = pl.BlockSpec(memory_space=pltpu.SMEM)


def params(mib):
    return pltpu.CompilerParams(vmem_limit_bytes=mib << 20)


CHUNKS = 4


def side_by_side(out_ref, rows, head, left, right):
    out_ref[head, rows] = jnp.concatenate([left[:, :HD], right[:, :HD]], axis=1)
    out_ref[head + 1, rows] = jnp.concatenate([left[:, HD:], right[:, HD:]], axis=1)


def pack_kernel(q_hbm, k_hbm, v_hbm, out_ref, q_ref, k_ref, v_ref, arrived):
    tokens, width = q_ref.shape
    step = width // CHUNKS
    copies = []
    for chunk in range(CHUNKS):
        columns = pl.ds(chunk * step, step)
        for place, (far, near) in enumerate(((k_hbm, k_ref), (v_hbm, v_ref), (q_hbm, q_ref))):
            copy = pltpu.make_async_copy(far.at[:, columns], near.at[:, columns], arrived.at[chunk, place])
            copy.start()
            copies.append(copy)
    half = tokens // 2
    for chunk in range(CHUNKS):
        for copy in copies[3 * chunk : 3 * chunk + 3]:
            copy.wait()
        for start in range(chunk * step, (chunk + 1) * step, WIDE):
            columns = pl.ds(start, WIDE)
            head = start // HD
            side_by_side(out_ref, pl.ds(0, tokens), head, k_ref[:, columns], v_ref[:, columns])
            upper, lower = q_ref[pl.ds(0, half), columns], q_ref[pl.ds(half, half), columns]
            side_by_side(out_ref, pl.ds(tokens, half), head, upper, lower)


def pack_heads(queries, keys, values):
    tokens, width = keys.shape
    held = pltpu.VMEM((tokens, width), keys.dtype)
    return pl.pallas_call(
        pack_kernel,
        out_shape=jax.ShapeDtypeStruct((HEADS, tokens + tokens // 2, WIDE), keys.dtype),
        in_specs=[pl.BlockSpec(memory_space=pl.ANY)] * 3,
        out_specs=VMEM,
        scratch_shapes=[held, held, held, pltpu.SemaphoreType.DMA((CHUNKS, 3))],
        compiler_params=params(60),
        name="pack_heads",
    )(queries, keys, values)


def unpack_kernel(x_ref, out_ref):
    half = x_ref.shape[1]
    for pair in range(HEADS // 2):
        even, odd = x_ref[2 * pair], x_ref[2 * pair + 1]
        columns = pl.ds(pair * WIDE, WIDE)
        out_ref[pl.ds(0, half), columns] = jnp.concatenate([even[:, :HD], odd[:, :HD]], axis=1)
        out_ref[pl.ds(half, half), columns] = jnp.concatenate([even[:, HD:], odd[:, HD:]], axis=1)


def unpack_heads(x):
    return pl.pallas_call(
        unpack_kernel,
        out_shape=jax.ShapeDtypeStruct((2 * x.shape[1], HEADS * HD), x.dtype),
        in_specs=[VMEM],
        out_specs=VMEM,
        compiler_params=params(16),
        name="unpack_heads",
    )(x)


def tile_scores(packed_ref, rows, half, keys):
    sources = TILE // QROWS
    queries = packed_ref[rows // QROWS : rows // QROWS + sources, 2 * QROWS :, half * HD : (half + 1) * HD]
    queries = queries.reshape(TILE, HD) * jnp.bfloat16(HD**-0.5)
    return lax.dot_general(queries, keys, (((1,), (1,)), ((), ())), preferred_element_type=jnp.float32)


def keys_and_values(kv):
    lane = lax.broadcasted_iota(jnp.int32, kv.shape, 1)
    return kv[:, :HD], jnp.where(lane < HD, jnp.bfloat16(1), kv)


def attend(packed_ref, kv_ref, old_peaks, store):
    keys, values = keys_and_values(kv_ref[...])
    units = [(rows, half) for rows in range(0, packed_ref.shape[0] * QROWS, TILE) for half in range(2)]

    def blend(rows, half, peak, old_peak, weights):
        store(rows, half, peak, old_peak, jnp.dot(weights, values, preferred_element_type=jnp.float32))

    scores = tile_scores(packed_ref, *units[0], keys)
    waiting = None
    for place, (rows, half) in enumerate(units):
        ahead = tile_scores(packed_ref, *units[place + 1], keys) if place + 1 < len(units) else None
        peak = jnp.max(scores, axis=1, keepdims=True)
        old_peak = None
        if old_peaks is not None:
            old_peak = old_peaks[half, pl.ds(rows, TILE)]
            peak = jnp.maximum(peak, old_peak)
        weights = jnp.exp(scores - peak[:, :1]).astype(jnp.bfloat16)
        if waiting is not None:
            blend(*waiting)
        waiting = (rows, half, peak, old_peak, weights)
        scores = ahead
    blend(*waiting)


def update(packed_ref, kv_ref, old_sums, old_peaks, sums, peaks):
    def store(rows, half, peak, old_peak, added):
        rows = pl.ds(rows, TILE)
        if old_peak is not None:
            added = old_sums[half, rows] * jnp.exp(old_peak - peak) + added
        sums[half, rows] = added
        peaks[half, rows] = jnp.broadcast_to(peak, (TILE, WIDE))

    attend(packed_ref, kv_ref, old_peaks, store)


def own_kernel(packed_ref, kv_ref, sums, peaks, mark):
    update(packed_ref, kv_ref, None, None, sums, peaks)
    mark[...] = jnp.zeros_like(mark)


def near_kernel(columns, mask_ref, packed_ref, one_ref, two_ref, _, sums, peaks):
    @pl.when(mask_ref[columns[0]] > 0)
    def _():
        update(packed_ref, one_ref, None, None, sums, peaks)

    @pl.when(mask_ref[columns[0]] <= 0)
    def _():
        sums[...] = jnp.zeros_like(sums)
        peaks[...] = jnp.full_like(peaks, LOWEST)

    @pl.when(mask_ref[columns[1]] > 0)
    def _():
        update(packed_ref, two_ref, sums, peaks, sums, peaks)


def far_kernel(
    columns, mask_ref, packed_ref, one_ref, two_ref, own_sums, own_peaks, near_sums, near_peaks, out_ref, sums, peaks
):
    @pl.when(mask_ref[columns[0]] > 0)
    def _():
        update(packed_ref, one_ref, near_sums, near_peaks, sums, peaks)

    @pl.when(mask_ref[columns[0]] <= 0)
    def _():
        sums[...] = near_sums[...]
        peaks[...] = near_peaks[...]

    def finish(rows, half, parts):
        parts = parts + [(own_sums[half, rows], own_peaks[half, rows]), (sums[half, rows], peaks[half, rows])]
        highest = functools.reduce(jnp.maximum, [part[1] for part in parts])
        total = sum(part[0] * jnp.exp(part[1] - highest) for part in parts)
        out_ref[rows, half * HD : (half + 1) * HD] = (total[:, HD:] / total[:, :HD]).astype(out_ref.dtype)

    def store(rows, half, peak, old_peak, added):
        finish(pl.ds(rows, TILE), half, [(added, jnp.broadcast_to(peak, added.shape))])

    @pl.when(mask_ref[columns[1]] > 0)
    def _():
        attend(packed_ref, two_ref, None, store)

    @pl.when(mask_ref[columns[1]] <= 0)
    def _():
        for start in range(0, out_ref.shape[0], TILE):
            for half in range(2):
                finish(pl.ds(start, TILE), half, [])


def cost(packed, blocks):
    pairs = blocks * (packed.shape[0] * 2 * QROWS) ** 2
    return pl.CostEstimate(flops=4 * pairs * HD, bytes_accessed=3 << 20, transcendentals=pairs)


def state_shape(packed):
    return jax.ShapeDtypeStruct((2, packed.shape[0] * QROWS, WIDE), jnp.float32)


def own_camera(packed, kv):
    return pl.pallas_call(
        own_kernel,
        out_shape=(state_shape(packed), state_shape(packed), jax.ShapeDtypeStruct((8, WIDE), jnp.float32)),
        in_specs=[VMEM, VMEM],
        out_specs=(VMEM, VMEM, VMEM),
        compiler_params=params(32),
        cost_estimate=cost(packed, 1),
        name="own_camera",
    )(packed, kv)


def near_cameras(columns, mask, packed, one, two, mark):
    return pl.pallas_call(
        functools.partial(near_kernel, columns),
        out_shape=(state_shape(packed), state_shape(packed)),
        in_specs=[SMEM] + [VMEM] * 4,
        out_specs=(VMEM, VMEM),
        compiler_params=params(32),
        cost_estimate=cost(packed, 2),
        name="near_cameras",
    )(mask, packed, one, two, mark)


def far_cameras(columns, mask, packed, one, two, own, near):
    state = pltpu.VMEM(near[0].shape, near[0].dtype)
    return pl.pallas_call(
        functools.partial(far_kernel, columns),
        out_shape=jax.ShapeDtypeStruct((near[0].shape[1], WIDE), packed.dtype),
        in_specs=[SMEM] + [VMEM] * 7,
        out_specs=VMEM,
        scratch_shapes=[state, state],
        compiler_params=params(32),
        cost_estimate=cost(packed, 2),
        name="far_cameras",
    )(mask, packed, one, two, *own, *near)


def swapped(array, first):
    cameras, places = lax.axis_size("cam"), lax.axis_size("seq")
    pairs = []
    for place in range(places):
        for camera in range((first + place) % 2, cameras, 2):
            one, two = camera * places + place, (camera + 1) % cameras * places + place
            pairs += [(one, two), (two, one)]
    return lax.ppermute(array, ("cam", "seq"), pairs)


def on_device(queries, keys, values, neighbour_mask):
    camera = lax.axis_index("cam")
    own_row = lax.dynamic_index_in_dim(neighbour_mask, camera, 0, keepdims=False)
    odd = (camera + lax.axis_index("seq")) % 2
    own_row = jnp.where(odd == 0, own_row, jnp.roll(own_row, 2))
    packed = pack_heads(queries[0], keys[0], values[0])
    packed = lax.all_to_all(packed, "seq", split_axis=0, concat_axis=0, tiled=True)
    kv = packed[:, : 2 * QROWS].reshape(-1, WIDE)
    one, two = swapped(kv, 0), swapped(kv, 1)
    *own, mark = own_camera(packed, kv)
    one, mark = lax.optimization_barrier((one, mark))
    far_two, far_one = swapped(one, 1), swapped(two, 0)
    near = near_cameras((0, 2), own_row, packed, one, two, mark)
    out = far_cameras((3, 1), own_row, packed, far_two, far_one, own, near)
    out = out.reshape(HEADS, QROWS, WIDE)
    out = lax.all_to_all(out, "seq", split_axis=0, concat_axis=0, tiled=True)
    return unpack_heads(out)[None]


def solution(mesh):
    return jax.shard_map(
        on_device,
        mesh=mesh,
        in_specs=(P("cam", "seq", None), P("cam", "seq", None), P("cam", "seq", None), P()),
        out_specs=P("cam", "seq", None),
        check_vma=False,
    )
```

```python
import functools

import jax
import jax.numpy as jnp
from jax import lax
from jax.experimental import pallas as pl
from jax.experimental.pallas import tpu as pltpu
from jax.sharding import PartitionSpec as P

HEADS = 32
HD = 64
WIDE = 2 * HD
TILE = 256
QROWS = 32
LOWEST = -1e30

VMEM = pl.BlockSpec(memory_space=pltpu.VMEM)
SMEM = pl.BlockSpec(memory_space=pltpu.SMEM)


def params(mib):
    return pltpu.CompilerParams(vmem_limit_bytes=mib << 20)


CHUNKS = 4


def side_by_side(out_ref, rows, head, left, right):
    out_ref[head, rows] = jnp.concatenate([left[:, :HD], right[:, :HD]], axis=1)
    out_ref[head + 1, rows] = jnp.concatenate([left[:, HD:], right[:, HD:]], axis=1)


def pack_kernel(q_hbm, k_hbm, v_hbm, out_ref, q_ref, k_ref, v_ref, arrived):
    tokens, width = q_ref.shape
    step = width // CHUNKS
    copies = []
    for chunk in range(CHUNKS):
        columns = pl.ds(chunk * step, step)
        for place, (far, near) in enumerate(((k_hbm, k_ref), (v_hbm, v_ref), (q_hbm, q_ref))):
            copy = pltpu.make_async_copy(far.at[:, columns], near.at[:, columns], arrived.at[chunk, place])
            copy.start()
            copies.append(copy)
    half = tokens // 2
    for chunk in range(CHUNKS):
        for copy in copies[3 * chunk : 3 * chunk + 3]:
            copy.wait()
        for start in range(chunk * step, (chunk + 1) * step, WIDE):
            columns = pl.ds(start, WIDE)
            head = start // HD
            side_by_side(out_ref, pl.ds(0, tokens), head, k_ref[:, columns], v_ref[:, columns])
            upper, lower = q_ref[pl.ds(0, half), columns], q_ref[pl.ds(half, half), columns]
            side_by_side(out_ref, pl.ds(tokens, half), head, upper, lower)


def pack_heads(queries, keys, values):
    tokens, width = keys.shape
    held = pltpu.VMEM((tokens, width), keys.dtype)
    return pl.pallas_call(
        pack_kernel,
        out_shape=jax.ShapeDtypeStruct((HEADS, tokens + tokens // 2, WIDE), keys.dtype),
        in_specs=[pl.BlockSpec(memory_space=pl.ANY)] * 3,
        out_specs=VMEM,
        scratch_shapes=[held, held, held, pltpu.SemaphoreType.DMA((CHUNKS, 3))],
        compiler_params=params(60),
        name="pack_heads",
    )(queries, keys, values)


def unpack_kernel(x_ref, out_ref):
    half = x_ref.shape[1]
    for pair in range(HEADS // 2):
        even, odd = x_ref[2 * pair], x_ref[2 * pair + 1]
        columns = pl.ds(pair * WIDE, WIDE)
        out_ref[pl.ds(0, half), columns] = jnp.concatenate([even[:, :HD], odd[:, :HD]], axis=1)
        out_ref[pl.ds(half, half), columns] = jnp.concatenate([even[:, HD:], odd[:, HD:]], axis=1)


def unpack_heads(x):
    return pl.pallas_call(
        unpack_kernel,
        out_shape=jax.ShapeDtypeStruct((2 * x.shape[1], HEADS * HD), x.dtype),
        in_specs=[VMEM],
        out_specs=VMEM,
        compiler_params=params(16),
        name="unpack_heads",
    )(x)


def tile_scores(packed_ref, rows, half, keys):
    sources = TILE // QROWS
    queries = packed_ref[rows // QROWS : rows // QROWS + sources, 2 * QROWS :, half * HD : (half + 1) * HD]
    queries = queries.reshape(TILE, HD) * jnp.bfloat16(HD**-0.5)
    return lax.dot_general(queries, keys, (((1,), (1,)), ((), ())), preferred_element_type=jnp.float32)


def keys_and_values(kv):
    lane = lax.broadcasted_iota(jnp.int32, kv.shape, 1)
    return kv[:, :HD], jnp.where(lane < HD, jnp.bfloat16(1), kv)


def attend(packed_ref, kv_ref, old_peaks, store):
    keys, values = keys_and_values(kv_ref[...])
    units = [(rows, half) for rows in range(0, packed_ref.shape[0] * QROWS, TILE) for half in range(2)]

    def blend(rows, half, peak, old_peak, weights):
        store(rows, half, peak, old_peak, jnp.dot(weights, values, preferred_element_type=jnp.float32))

    scores = tile_scores(packed_ref, *units[0], keys)
    waiting = None
    for place, (rows, half) in enumerate(units):
        ahead = tile_scores(packed_ref, *units[place + 1], keys) if place + 1 < len(units) else None
        peak = jnp.max(scores, axis=1, keepdims=True)
        old_peak = None
        if old_peaks is not None:
            old_peak = old_peaks[half, pl.ds(rows, TILE)]
            peak = jnp.maximum(peak, old_peak)
        weights = jnp.exp(scores - peak[:, :1]).astype(jnp.bfloat16)
        if waiting is not None:
            blend(*waiting)
        waiting = (rows, half, peak, old_peak, weights)
        scores = ahead
    blend(*waiting)


def update(packed_ref, kv_ref, old_sums, old_peaks, sums, peaks):
    def store(rows, half, peak, old_peak, added):
        rows = pl.ds(rows, TILE)
        if old_peak is not None:
            added = old_sums[half, rows] * jnp.exp(old_peak - peak) + added
        sums[half, rows] = added
        peaks[half, rows] = jnp.broadcast_to(peak, (TILE, WIDE))

    attend(packed_ref, kv_ref, old_peaks, store)


def own_kernel(packed_ref, kv_ref, sums, peaks, mark):
    update(packed_ref, kv_ref, None, None, sums, peaks)
    mark[...] = jnp.zeros_like(mark)


def enabled(mask_ref, step):
    camera = lax.axis_index("cam")
    odd = lax.rem(camera + lax.axis_index("seq"), 2)
    ahead, behind = step - 1 + 2 * odd, step + 1 - 2 * odd
    return mask_ref[camera, ahead] > 0, mask_ref[camera, behind] > 0


def near_kernel(step, mask_ref, packed_ref, one_ref, two_ref, _, sums, peaks):
    first, second = enabled(mask_ref, step)

    @pl.when(first)
    def _():
        update(packed_ref, one_ref, None, None, sums, peaks)

    @pl.when(jnp.logical_not(first))
    def _():
        sums[...] = jnp.zeros_like(sums)
        peaks[...] = jnp.full_like(peaks, LOWEST)

    @pl.when(second)
    def _():
        update(packed_ref, two_ref, sums, peaks, sums, peaks)


def far_kernel(
    step, mask_ref, packed_ref, one_ref, two_ref, own_sums, own_peaks, near_sums, near_peaks, out_ref, sums, peaks
):
    second, first = enabled(mask_ref, step)

    @pl.when(first)
    def _():
        update(packed_ref, one_ref, near_sums, near_peaks, sums, peaks)

    @pl.when(jnp.logical_not(first))
    def _():
        sums[...] = near_sums[...]
        peaks[...] = near_peaks[...]

    def finish(rows, half, parts):
        parts = parts + [(own_sums[half, rows], own_peaks[half, rows]), (sums[half, rows], peaks[half, rows])]
        highest = functools.reduce(jnp.maximum, [part[1] for part in parts])
        total = sum(part[0] * jnp.exp(part[1] - highest) for part in parts)
        out_ref[rows, half * HD : (half + 1) * HD] = (total[:, HD:] / total[:, :HD]).astype(out_ref.dtype)

    def store(rows, half, peak, old_peak, added):
        finish(pl.ds(rows, TILE), half, [(added, jnp.broadcast_to(peak, added.shape))])

    @pl.when(second)
    def _():
        attend(packed_ref, two_ref, None, store)

    @pl.when(jnp.logical_not(second))
    def _():
        for start in range(0, out_ref.shape[0], TILE):
            for half in range(2):
                finish(pl.ds(start, TILE), half, [])


def cost(packed, blocks):
    pairs = blocks * (packed.shape[0] * 2 * QROWS) ** 2
    return pl.CostEstimate(flops=4 * pairs * HD, bytes_accessed=3 << 20, transcendentals=pairs)


def state_shape(packed):
    return jax.ShapeDtypeStruct((2, packed.shape[0] * QROWS, WIDE), jnp.float32)


def own_camera(packed, kv):
    return pl.pallas_call(
        own_kernel,
        out_shape=(state_shape(packed), state_shape(packed), jax.ShapeDtypeStruct((8, WIDE), jnp.float32)),
        in_specs=[VMEM, VMEM],
        out_specs=(VMEM, VMEM, VMEM),
        compiler_params=params(32),
        cost_estimate=cost(packed, 1),
        name="own_camera",
    )(packed, kv)


def near_cameras(step, mask, packed, one, two, mark):
    return pl.pallas_call(
        functools.partial(near_kernel, step),
        out_shape=(state_shape(packed), state_shape(packed)),
        in_specs=[SMEM] + [VMEM] * 4,
        out_specs=(VMEM, VMEM),
        compiler_params=params(32),
        cost_estimate=cost(packed, 2),
        name="near_cameras",
    )(mask, packed, one, two, mark)


def far_cameras(step, mask, packed, one, two, own, near):
    state = pltpu.VMEM(near[0].shape, near[0].dtype)
    return pl.pallas_call(
        functools.partial(far_kernel, step),
        out_shape=jax.ShapeDtypeStruct((near[0].shape[1], WIDE), packed.dtype),
        in_specs=[SMEM] + [VMEM] * 7,
        out_specs=VMEM,
        scratch_shapes=[state, state],
        compiler_params=params(32),
        cost_estimate=cost(packed, 2),
        name="far_cameras",
    )(mask, packed, one, two, *own, *near)


def swapped(array, first):
    cameras, places = lax.axis_size("cam"), lax.axis_size("seq")
    pairs = []
    for place in range(places):
        for camera in range((first + place) % 2, cameras, 2):
            one, two = camera * places + place, (camera + 1) % cameras * places + place
            pairs += [(one, two), (two, one)]
    return lax.ppermute(array, ("cam", "seq"), pairs)


def on_device(queries, keys, values, neighbour_mask):
    packed = pack_heads(queries[0], keys[0], values[0])
    packed = lax.all_to_all(packed, "seq", split_axis=0, concat_axis=0, tiled=True)
    kv = packed[:, : 2 * QROWS].reshape(-1, WIDE)
    one, two = swapped(kv, 0), swapped(kv, 1)
    *own, mark = own_camera(packed, kv)
    one, mark = lax.optimization_barrier((one, mark))
    far_two, far_one = swapped(one, 1), swapped(two, 0)
    near = near_cameras(1, neighbour_mask, packed, one, two, mark)
    out = far_cameras(2, neighbour_mask, packed, far_two, far_one, own, near)
    out = out.reshape(HEADS, QROWS, WIDE)
    out = lax.all_to_all(out, "seq", split_axis=0, concat_axis=0, tiled=True)
    return unpack_heads(out)[None]


def solution(mesh):
    return jax.shard_map(
        on_device,
        mesh=mesh,
        in_specs=(P("cam", "seq", None), P("cam", "seq", None), P("cam", "seq", None), P()),
        out_specs=P("cam", "seq", None),
        check_vma=False,
    )
```
